32 devices in a mesh: group: 2 (over y), freq: 4 (over z), recv: 2 (over x), sub: 2 (over core).
Axes of the slice: x: 2, y: 2, z: 4, core: 2. Of those that a mesh axis runs over, the one named last changes fastest.
Arguments:
- focusing: float32 [8, 512, 8192], P(('group', 'sub'), 'freq', 'recv'), parts along dimension 0, may hold values from -6 to 6
- observed: float32 [8, 512, 8192], P(('group', 'sub'), 'freq', 'recv'), parts along dimension 0, may hold values from -6 to 6
- recv_factor: bfloat16 [4, 4, 16, 32, 8192], P('group', 'freq', 'sub', None, 'recv'), parts along dimension 0, may hold values from -0.0625 to 0.0625
- source_factor: bfloat16 [4, 4, 16, 32, 8192], P('group', 'freq', 'sub', 'recv'), parts along dimension 0, may hold values from -1.5 to 1.5
- tile_ranks: int32 [8, 32, 32], P(('group', 'freq'), 'recv'), parts along dimension 0, may hold values from 1 to 16
- window_start: int32 [8, 8192], P(('group', 'sub'), 'recv'), parts along dimension 0, may hold values from 0 to 255
- window_end: int32 [8, 8192], P(('group', 'sub'), 'recv'), parts along dimension 0, may hold values from 64 to 512, as said below
Outputs:
- new_focusing: float32 [8, 512, 8192], P(('group', 'sub'), 'freq', 'recv'), parts along dimension 0
- new_residual: float32 [8, 512, 8192], P(('group', 'sub'), 'freq', 'recv'), parts along dimension 0
The draws below stay inside these ranges and needn't reach their ends.
There are 2 independent parts, one for each index of `group`. The reference program is written for one: setup_inputs(seed, part) draws one part's arguments, and reference() takes and returns one part's arrays. A program takes and returns all parts, laid end to end along the dimension named above; each array names one. Nothing has to cross between parts.
Inputs may be any that keep to these rules, and one draw needn't show every extreme that they name: `window_end`: always above window_start.
All inputs are finite; a program needn't handle non-finite values.
Results may differ from the reference program's by a relative error of at most 0.005.
Values may be sent and summed in bfloat16 or wider, within the bound.
A program may use at most 192 MiB of HBM per device.

```python
import math
import jax
import jax.numpy as jnp
from jax import lax

NREC = 8192
NT = 512
NB = 256
KMAX = 16
FOC = 4
NF = 4
NTILE = 32


def window_pair(key):
    key_start, key_span = jax.random.split(key)
    start_idx = jnp.maximum(jax.random.randint(key_start, (FOC, NREC), -(NT // 4), NT // 2), 0)
    span_len = jax.random.randint(key_span, (FOC, NREC), NT // 8, NT)
    return (start_idx.astype(jnp.int32), jnp.minimum(start_idx + span_len, NT).astype(jnp.int32))


def draw_window_start(key, part):
    paired = window_pair(key)
    return paired[0]


def draw_window_end(key, part):
    paired = window_pair(key)
    return paired[1]


def place_ends(array, own_key, least, top_value):
    dims = array.shape
    index_at = [jax.random.randint(jax.random.fold_in(own_key, axis), (), 0, dims[axis]) for axis in range(len(dims))]
    array = array.at[tuple(index_at)].set(least)
    longest = dims.index(max(dims))
    index_at[longest] = (index_at[longest] + 1) % dims[longest]
    return array.at[tuple(index_at)].set(top_value)


def levels(key, shape, cuts, smallest, largest):
    def one(position, blocks):
        draws = jax.random.uniform(jax.random.fold_in(jax.random.fold_in(key, 6), position), (blocks,), jnp.float32, smallest / len(cuts), largest / len(cuts))
        return jnp.repeat(jnp.exp(draws), shape[position] // blocks).reshape((-1,) + (1,) * (len(shape) - position - 1))

    level = one(*cuts[0])
    for cut in cuts[1:]:
        level = level * one(*cut)
    return level


def gaussian(rng, dims, deviation, reach, cuts=(), held_as=jnp.bfloat16):
    factor_of = levels(rng, dims, cuts, -0.22, 0.18) if cuts else 1.0
    array = jax.random.normal(rng, dims, jnp.float32) * deviation * factor_of
    return jnp.minimum(jnp.maximum(array, -reach), reach).astype(held_as)


def setup_inputs(seed: int = 0, part: int = 0) -> dict:
    keys = jax.random.split(jax.random.key(seed), 8)
    part_keys = jax.random.split(jax.random.fold_in(keys[7], part), 8)
    focusing = gaussian(part_keys[0], (FOC, NT, NREC), 1.0, 6.0, ((0, 2), (1, 4), (2, 2)), jnp.float32)
    observed = gaussian(part_keys[1], (FOC, NT, NREC), 1.0, 6.0, ((0, 2), (1, 4), (2, 2)), jnp.float32)
    recv_factor = gaussian(part_keys[2], (2, NF, KMAX, NTILE, NREC), NREC ** -0.5, 0.0625, ((1, 4), (2, 2), (4, 2)))
    source_factor = gaussian(part_keys[3], (2, NF, KMAX, NTILE, NREC), KMAX ** -0.5, 1.5, ((1, 4), (2, 2), (3, 2)))
    tile_ranks = place_ends(jax.random.randint(part_keys[4], (NF, NTILE, NTILE), 1, KMAX + 1), jax.random.fold_in(part_keys[4], 1), 1, KMAX).astype(jnp.int32)
    window_start = draw_window_start(jax.random.fold_in(jax.random.fold_in(keys[7], part), 71), part)
    window_end = draw_window_end(jax.random.fold_in(jax.random.fold_in(keys[7], part), 71), part)
    return dict(focusing=focusing, observed=observed, recv_factor=recv_factor, source_factor=source_factor, tile_ranks=tile_ranks, window_start=window_start, window_end=window_end)


first_bin = 4
relax_step = 1.0
highest = lax.Precision.HIGHEST


def dft_tables(count, samples):
    freqs = first_bin + jnp.arange(count, dtype=jnp.int32)
    sample_ids = jnp.arange(samples, dtype=jnp.int32)
    turns = ((freqs[:, None] * sample_ids[None, :]) % samples).astype(jnp.float32)
    phase = turns * (2.0 * math.pi / samples)
    weight = float(count * samples) ** -0.25
    return jnp.cos(phase) * weight, jnp.sin(phase) * weight


def rounded(values):
    return lax.optimization_barrier(values.astype(jnp.bfloat16)).astype(jnp.float32)


def spectrum_of(signal, cos_table, sin_table):
    real_part = jnp.einsum("ft,qtr->fqr", cos_table, signal, precision=highest)
    imag_part = -jnp.einsum("ft,qtr->fqr", sin_table, signal, precision=highest)
    return rounded(jnp.stack([real_part, imag_part]))


def signal_of(spectrum, cos_table, sin_table):
    return (jnp.einsum("ft,fqr->qtr", cos_table, spectrum[0], precision=highest)
            - jnp.einsum("ft,fqr->qtr", sin_table, spectrum[1], precision=highest))


def forward(spectrum, recv_parts, source_parts, rank_keep):
    tiles = spectrum.reshape(2, NF, FOC, NTILE, NB)
    real_part = (jnp.einsum("fkjin,fqin->fkjiq", recv_parts[0], tiles[0], precision=highest)
                 - jnp.einsum("fkjin,fqin->fkjiq", recv_parts[1], tiles[1], precision=highest))
    imag_part = (jnp.einsum("fkjin,fqin->fkjiq", recv_parts[0], tiles[1], precision=highest)
                 + jnp.einsum("fkjin,fqin->fkjiq", recv_parts[1], tiles[0], precision=highest))
    coeffs = rounded(jnp.stack([real_part, imag_part]) * rank_keep[None, :, :, :, :, None])
    out_real = (jnp.einsum("fkijn,fkjiq->fqjn", source_parts[0], coeffs[0], precision=highest)
                - jnp.einsum("fkijn,fkjiq->fqjn", source_parts[1], coeffs[1], precision=highest))
    out_imag = (jnp.einsum("fkijn,fkjiq->fqjn", source_parts[0], coeffs[1], precision=highest)
                + jnp.einsum("fkijn,fkjiq->fqjn", source_parts[1], coeffs[0], precision=highest))
    return jnp.stack([out_real, out_imag]).reshape(2, NF, FOC, NREC)


def adjoint(spectrum, recv_parts, source_parts, rank_keep):
    tiles = spectrum.reshape(2, NF, FOC, NTILE, NB)
    real_part = (jnp.einsum("fkijn,fqjn->fkjiq", source_parts[0], tiles[0], precision=highest)
                 + jnp.einsum("fkijn,fqjn->fkjiq", source_parts[1], tiles[1], precision=highest))
    imag_part = (jnp.einsum("fkijn,fqjn->fkjiq", source_parts[0], tiles[1], precision=highest)
                 - jnp.einsum("fkijn,fqjn->fkjiq", source_parts[1], tiles[0], precision=highest))
    coeffs = rounded(jnp.stack([real_part, imag_part]) * rank_keep[None, :, :, :, :, None])
    out_real = (jnp.einsum("fkjin,fkjiq->fqin", recv_parts[0], coeffs[0], precision=highest)
                + jnp.einsum("fkjin,fkjiq->fqin", recv_parts[1], coeffs[1], precision=highest))
    out_imag = (jnp.einsum("fkjin,fkjiq->fqin", recv_parts[0], coeffs[1], precision=highest)
                - jnp.einsum("fkjin,fkjiq->fqin", recv_parts[1], coeffs[0], precision=highest))
    return jnp.stack([out_real, out_imag]).reshape(2, NF, FOC, NREC)


def reference(focusing, observed, recv_factor, source_factor, tile_ranks, window_start, window_end):
    cos_table, sin_table = dft_tables(NF, NT)
    recv_parts = recv_factor.astype(jnp.float32).reshape(2, NF, KMAX, NTILE, NTILE, NB)
    source_parts = source_factor.astype(jnp.float32).reshape(2, NF, KMAX, NTILE, NTILE, NB)
    rank_ids = jnp.arange(KMAX, dtype=jnp.int32)
    rank_keep = (rank_ids[None, :, None, None] < jnp.transpose(tile_ranks, (0, 2, 1))[:, None, :, :]).astype(jnp.float32)
    sample_ids = jnp.arange(NT, dtype=jnp.int32)
    window = ((window_start[:, None, :] <= sample_ids[None, :, None])
              & (sample_ids[None, :, None] < window_end[:, None, :])).astype(jnp.float32)
    predicted = signal_of(forward(spectrum_of(focusing, cos_table, sin_table), recv_parts, source_parts, rank_keep), cos_table, sin_table)
    residual = observed - window * predicted
    gradient = signal_of(adjoint(spectrum_of(window * residual, cos_table, sin_table), recv_parts, source_parts, rank_keep), cos_table, sin_table)
    image = window * signal_of(forward(spectrum_of(gradient, cos_table, sin_table), recv_parts, source_parts, rank_keep), cos_table, sin_table)
    return focusing + relax_step * gradient, residual - relax_step * image
```

```python
import math

import jax
import jax.numpy as jnp
from jax import lax
from jax.sharding import PartitionSpec as P

NT = 512


first_bin = 4
relax_step = 1.0
highest = lax.Precision.HIGHEST


def dft_tables(count, samples):
    freqs = first_bin + jnp.arange(count, dtype=jnp.int32)
    sample_ids = jnp.arange(samples, dtype=jnp.int32)
    turns = (freqs[:, None] * sample_ids[None, :] % samples).astype(jnp.float32)
    phase = turns * (2.0 * math.pi / samples)
    weight = float(count * samples) ** (-0.25)
    return (jnp.cos(phase) * weight, jnp.sin(phase) * weight)


def signal_of(spectrum, cos_table, sin_table):
    return jnp.einsum("ft,fqr->qtr", cos_table, spectrum[0], precision=highest) - jnp.einsum(
        "ft,fqr->qtr", sin_table, spectrum[1], precision=highest
    )


def contract(form, left, right):
    return jnp.einsum(form, left, right, preferred_element_type=jnp.float32)


def body(focusing, observed, recv_factor, source_factor, tile_ranks, window_start, window_end):
    freq_count = lax.axis_size("freq")
    recv_count = lax.axis_size("recv")
    sub_count = lax.axis_size("sub")
    bands = recv_factor.shape[1]
    rank_cols = recv_factor.shape[2]
    tiles_all = recv_factor.shape[3]
    tiles_here = source_factor.shape[3]
    half_foc, local_t, rec_block = focusing.shape
    tile_len = rec_block // tiles_here
    col_tiles = tiles_all // recv_count
    cos_table, sin_table = dft_tables(bands * freq_count, NT)
    rank_ids = lax.axis_index("sub") * rank_cols + jnp.arange(rank_cols, dtype=jnp.int32)
    rank_keep = (
        rank_ids[None, :, None, None] < jnp.transpose(tile_ranks, (0, 2, 1))[:, None, :, :]
    ).astype(jnp.float32)
    recv_tiles = recv_factor.reshape(2, bands, rank_cols, tiles_all, tiles_here, tile_len)
    recv_blocks = recv_factor.reshape(
        2, bands, rank_cols, recv_count, col_tiles, tiles_here, tile_len
    )
    source_blocks = source_factor.reshape(
        2, bands, rank_cols, tiles_here, recv_count, col_tiles, tile_len
    )
    keep_blocks = rank_keep.reshape(bands, rank_cols, recv_count, col_tiles, tiles_here)

    def forward(spec_half):
        gathered = lax.all_gather(spec_half, "sub", axis=2, tiled=True)
        tiles = gathered.reshape(2, bands, sub_count * half_foc, tiles_here, tile_len)
        real_part = contract("fkjin,fqin->fkjiq", recv_tiles[0], tiles[0]) - contract(
            "fkjin,fqin->fkjiq", recv_tiles[1], tiles[1]
        )
        imag_part = contract("fkjin,fqin->fkjiq", recv_tiles[0], tiles[1]) + contract(
            "fkjin,fqin->fkjiq", recv_tiles[1], tiles[0]
        )
        coeffs = (jnp.stack([real_part, imag_part]) * rank_keep[None, :, :, :, :, None]).astype(
            jnp.bfloat16
        )
        coeffs = coeffs.reshape(
            2, bands, rank_cols, recv_count, col_tiles, tiles_here, sub_count, half_foc
        )
        out_real = contract("fkibjn,fkbjiud->fbudjn", source_blocks[0], coeffs[0]) - contract(
            "fkibjn,fkbjiud->fbudjn", source_blocks[1], coeffs[1]
        )
        out_imag = contract("fkibjn,fkbjiud->fbudjn", source_blocks[0], coeffs[1]) + contract(
            "fkibjn,fkbjiud->fbudjn", source_blocks[1], coeffs[0]
        )
        partial_term = jnp.stack([out_real, out_imag]).reshape(
            2, bands, recv_count * sub_count * half_foc, rec_block
        )
        return lax.psum_scatter(partial_term, ("recv", "sub"), scatter_dimension=2, tiled=True)

    traces, seen = (focusing, observed)
    sample_ids = lax.axis_index("freq") * local_t + jnp.arange(local_t, dtype=jnp.int32)
    window = (
        (window_start[:, None, :] <= sample_ids[None, :, None])
        & (sample_ids[None, :, None] < window_end[:, None, :])
    ).astype(jnp.float32)

    local_cos = lax.dynamic_slice_in_dim(cos_table, lax.axis_index("freq") * local_t, local_t, 1)
    local_sin = lax.dynamic_slice_in_dim(sin_table, lax.axis_index("freq") * local_t, local_t, 1)

    def to_spectrum(signal):
        real_part = jnp.einsum("ft,qtr->fqr", local_cos, signal, precision=highest)
        imag_part = -jnp.einsum("ft,qtr->fqr", local_sin, signal, precision=highest)
        whole = lax.psum_scatter(
            jnp.stack([real_part, imag_part]), "freq", scatter_dimension=1, tiled=True
        )
        return whole.astype(jnp.bfloat16)

    def to_signal(spectrum):
        return signal_of(
            lax.all_gather(spectrum, "freq", axis=1, tiled=True), local_cos, local_sin
        )

    predicted = to_signal(forward(to_spectrum(traces)))
    residual = seen - window * predicted
    gathered = lax.all_gather(to_spectrum(window * residual), ("recv", "sub"), axis=2, tiled=True)
    tiles = gathered.reshape(2, bands, recv_count, sub_count, half_foc, col_tiles, tile_len)
    real_part = contract("fkibjn,fbudjn->fkbjiud", source_blocks[0], tiles[0]) + contract(
        "fkibjn,fbudjn->fkbjiud", source_blocks[1], tiles[1]
    )
    imag_part = contract("fkibjn,fbudjn->fkbjiud", source_blocks[0], tiles[1]) - contract(
        "fkibjn,fbudjn->fkbjiud", source_blocks[1], tiles[0]
    )
    coeffs = (
        jnp.stack([real_part, imag_part]) * keep_blocks[None, :, :, :, :, :, None, None]
    ).astype(jnp.bfloat16)
    out_real = contract("fkbjim,fkbjiud->fudim", recv_blocks[0], coeffs[0]) + contract(
        "fkbjim,fkbjiud->fudim", recv_blocks[1], coeffs[1]
    )
    out_imag = contract("fkbjim,fkbjiud->fudim", recv_blocks[0], coeffs[1]) - contract(
        "fkbjim,fkbjiud->fudim", recv_blocks[1], coeffs[0]
    )
    partial_term = jnp.stack([out_real, out_imag]).reshape(
        2, bands, sub_count * half_foc, rec_block
    )
    grad_spec = lax.psum_scatter(partial_term, "sub", scatter_dimension=2, tiled=True)
    gradient = to_signal(grad_spec)
    gain = (0.5 * NT) * float(bands * freq_count * NT) ** (-0.5)
    image = window * to_signal(forward((grad_spec * gain).astype(jnp.bfloat16)))
    new_focus = traces + relax_step * gradient
    new_residual = residual - relax_step * image
    return (new_focus, new_residual)


def solution(mesh):
    placed = (
        P(("group", "sub"), "freq", "recv"),
        P(("group", "sub"), "freq", "recv"),
        P("group", "freq", "sub", None, "recv"),
        P("group", "freq", "sub", "recv", None),
        P(("group", "freq"), "recv", None),
        P(("group", "sub"), "recv"),
        P(("group", "sub"), "recv"),
    )
    return jax.shard_map(
        body,
        mesh=mesh,
        in_specs=placed,
        out_specs=(P(("group", "sub"), "freq", "recv"), P(("group", "sub"), "freq", "recv")),
        check_vma=False,
    )
```

```python
import functools
import math

import jax
import jax.numpy as jnp
from jax import lax
from jax.experimental import pallas as pl
from jax.experimental.pallas import tpu as pltpu
from jax.sharding import PartitionSpec as P

NT = 512


first_bin = 4
relax_step = 1.0
highest = lax.Precision.HIGHEST


def dft_tables(count, samples):
    freqs = first_bin + jnp.arange(count, dtype=jnp.int32)
    sample_ids = jnp.arange(samples, dtype=jnp.int32)
    turns = (freqs[:, None] * sample_ids[None, :] % samples).astype(jnp.float32)
    phase = turns * (2.0 * math.pi / samples)
    weight = float(count * samples) ** (-0.25)
    return (jnp.cos(phase) * weight, jnp.sin(phase) * weight)


def signal_of(spectrum, cos_table, sin_table):
    return jnp.einsum("ft,fqr->qtr", cos_table, spectrum[0], precision=highest) - jnp.einsum(
        "ft,fqr->qtr", sin_table, spectrum[1], precision=highest
    )


def contract(form, left, right):
    return jnp.einsum(form, left, right, preferred_element_type=jnp.float32)


def body(focusing, observed, recv_factor, source_factor, tile_ranks, window_start, window_end):
    freq_count = lax.axis_size("freq")
    recv_count = lax.axis_size("recv")
    sub_count = lax.axis_size("sub")
    bands = recv_factor.shape[1]
    rank_cols = recv_factor.shape[2]
    tiles_all = recv_factor.shape[3]
    tiles_here = source_factor.shape[3]
    half_foc, local_t, rec_block = focusing.shape
    tile_len = rec_block // tiles_here
    col_tiles = tiles_all // recv_count
    cos_table, sin_table = dft_tables(bands * freq_count, NT)
    rank_ids = lax.axis_index("sub") * rank_cols + jnp.arange(rank_cols, dtype=jnp.int32)
    rank_keep = (
        rank_ids[None, :, None, None] < jnp.transpose(tile_ranks, (0, 2, 1))[:, None, :, :]
    ).astype(jnp.float32)
    recv_tiles = recv_factor.reshape(2, bands, rank_cols, tiles_all, tiles_here, tile_len)
    recv_blocks = recv_factor.reshape(
        2, bands, rank_cols, recv_count, col_tiles, tiles_here, tile_len
    )
    source_blocks = source_factor.reshape(
        2, bands, rank_cols, tiles_here, recv_count, col_tiles, tile_len
    )
    keep_blocks = rank_keep.reshape(bands, rank_cols, recv_count, col_tiles, tiles_here)

    def forward(spec_half):
        gathered = lax.all_gather(spec_half, "sub", axis=2, tiled=True)
        tiles = gathered.reshape(2, bands, sub_count * half_foc, tiles_here, tile_len)
        real_part = contract("fkjin,fqin->fkjiq", recv_tiles[0], tiles[0]) - contract(
            "fkjin,fqin->fkjiq", recv_tiles[1], tiles[1]
        )
        imag_part = contract("fkjin,fqin->fkjiq", recv_tiles[0], tiles[1]) + contract(
            "fkjin,fqin->fkjiq", recv_tiles[1], tiles[0]
        )
        coeffs = (jnp.stack([real_part, imag_part]) * rank_keep[None, :, :, :, :, None]).astype(
            jnp.bfloat16
        )
        coeffs = coeffs.reshape(
            2, bands, rank_cols, recv_count, col_tiles, tiles_here, sub_count, half_foc
        )
        out_real = contract("fkibjn,fkbjiud->fbudjn", source_blocks[0], coeffs[0]) - contract(
            "fkibjn,fkbjiud->fbudjn", source_blocks[1], coeffs[1]
        )
        out_imag = contract("fkibjn,fkbjiud->fbudjn", source_blocks[0], coeffs[1]) + contract(
            "fkibjn,fkbjiud->fbudjn", source_blocks[1], coeffs[0]
        )
        partial_term = jnp.stack([out_real, out_imag]).reshape(
            2, bands, recv_count * sub_count * half_foc, rec_block
        )
        return lax.psum_scatter(partial_term, ("recv", "sub"), scatter_dimension=2, tiled=True)

    traces, seen = (focusing, observed)
    sample_ids = lax.axis_index("freq") * local_t + jnp.arange(local_t, dtype=jnp.int32)
    window = (
        (window_start[:, None, :] <= sample_ids[None, :, None])
        & (sample_ids[None, :, None] < window_end[:, None, :])
    ).astype(jnp.float32)

    local_cos = lax.dynamic_slice_in_dim(cos_table, lax.axis_index("freq") * local_t, local_t, 1)
    local_sin = lax.dynamic_slice_in_dim(sin_table, lax.axis_index("freq") * local_t, local_t, 1)

    def to_spectrum(signal):
        real_part = jnp.einsum("ft,qtr->fqr", local_cos, signal, precision=highest)
        imag_part = -jnp.einsum("ft,qtr->fqr", local_sin, signal, precision=highest)
        whole = lax.psum_scatter(
            jnp.stack([real_part, imag_part]), "freq", scatter_dimension=1, tiled=True
        )
        return whole.astype(jnp.bfloat16)

    def to_signal(spectrum):
        return signal_of(
            lax.all_gather(spectrum, "freq", axis=1, tiled=True), local_cos, local_sin
        )

    predicted = to_signal(forward(to_spectrum(traces)))
    residual = seen - window * predicted
    gathered = lax.all_gather(to_spectrum(window * residual), ("recv", "sub"), axis=2, tiled=True)
    tiles = gathered.reshape(2, bands, recv_count, sub_count, half_foc, col_tiles, tile_len)
    real_part = contract("fkibjn,fbudjn->fkbjiud", source_blocks[0], tiles[0]) + contract(
        "fkibjn,fbudjn->fkbjiud", source_blocks[1], tiles[1]
    )
    imag_part = contract("fkibjn,fbudjn->fkbjiud", source_blocks[0], tiles[1]) - contract(
        "fkibjn,fbudjn->fkbjiud", source_blocks[1], tiles[0]
    )
    coeffs = (
        jnp.stack([real_part, imag_part]) * keep_blocks[None, :, :, :, :, :, None, None]
    ).astype(jnp.bfloat16)
    out_real = contract("fkbjim,fkbjiud->fudim", recv_blocks[0], coeffs[0]) + contract(
        "fkbjim,fkbjiud->fudim", recv_blocks[1], coeffs[1]
    )
    out_imag = contract("fkbjim,fkbjiud->fudim", recv_blocks[0], coeffs[1]) - contract(
        "fkbjim,fkbjiud->fudim", recv_blocks[1], coeffs[0]
    )
    partial_term = jnp.stack([out_real, out_imag]).reshape(
        2, bands, sub_count * half_foc, rec_block
    )
    grad_spec = lax.psum_scatter(partial_term, "sub", scatter_dimension=2, tiled=True)
    gradient = to_signal(grad_spec)
    gain = (0.5 * NT) * float(bands * freq_count * NT) ** (-0.5)
    image = window * to_signal(forward((grad_spec * gain).astype(jnp.bfloat16)))
    new_focus = traces + relax_step * gradient
    new_residual = residual - relax_step * image
    return (new_focus, new_residual)


CHUNK = 512


def dot(a, b):
    return lax.dot_general(a, b, (((1,), (0,)), ((), ())), preferred_element_type=jnp.float32)


def dot_nt(a, b):
    return lax.dot_general(a, b, (((1,), (1,)), ((), ())), preferred_element_type=jnp.float32)


def turned(x, sign):
    row = lax.broadcasted_iota(jnp.int32, x.shape, 0)
    up = pltpu.roll(x, x.shape[0] - 1, 0)
    down = pltpu.roll(x, 1, 0)
    return jnp.where(row % 2 == 0, -sign * up, sign * down)


def halves(x):
    high = x.astype(jnp.bfloat16)
    return high, (x - high.astype(jnp.float32)).astype(jnp.bfloat16)


def spectrum_chunk(table_wide, v):
    out = dot(table_wide, jnp.concatenate(halves(v), axis=0))
    rows = out.shape[0] // 2
    return out[:rows] + out[rows:]


def signal_chunk(table_tall, p):
    high, low = halves(p)
    high, low = high.astype(jnp.float32), low.astype(jnp.float32)
    return dot(table_tall, jnp.concatenate([high, low, high, low], axis=0).astype(jnp.bfloat16))


def seen_rows(ref, d, lanes, count):
    return jnp.concatenate([ref[f, 2 * d : 2 * d + 2, lanes] for f in range(count)], axis=0)


def core_kernel(
    nf, tiles, tiles_here, ranks, tile_len, gain,
    foc, obs, uf, vf, keep_f, keep_a, start, end, tids, table_wide, table_tall,
    p_out, g_out,
    sp, zrecv, zsum, zother, coef, ybuf, yrecv, pg, zg, adj, ga, gother, gg,
    send_sem, recv_sem,
):
    z, x, c = lax.axis_index("freq"), lax.axis_index("recv"), lax.axis_index("sub")
    lanes_all = tiles_here * tile_len
    peers = [(dx, dc) for dx in range(2) for dc in range(2) if dx + dc]
    zs = [{"freq": lax.rem(z + k, nf)} for k in range(1, nf)]
    near = [{"recv": x + dx - 2 * dx * x, "sub": c + dc - 2 * dc * c} for dx, dc in peers]
    barrier = pltpu.get_barrier_semaphore()
    for device in zs + near:
        pl.semaphore_signal(
            barrier, inc=1, device_id=device, device_id_type=pl.DeviceIdType.MESH
        )
    pl.semaphore_wait(barrier, nf - 1 + len(peers))
    used = [0]

    def send(src, dst, device):
        n = used[0]
        used[0] += 1
        copy = pltpu.make_async_remote_copy(
            src_ref=src, dst_ref=dst, send_sem=send_sem.at[n], recv_sem=recv_sem.at[n],
            device_id=device, device_id_type=pl.DeviceIdType.MESH,
        )
        copy.start()
        return copy

    def reduce_freq(n):
        copies = [
            send(sp.at[n, zs[k]["freq"]], zrecv.at[n, k], zs[k]) for k in range(nf - 1)
        ]
        for copy in copies:
            copy.wait()
        total = sp[n, z]
        for k in range(nf - 1):
            total = total + zrecv[n, k]
        return total

    def gather_freq(buf):
        return [send(buf.at[z], buf.at[z], zs[k]) for k in range(nf - 1)]

    def put_spectrum(n, d, lanes, out):
        for f in range(nf):
            sp[n, f, 2 * d : 2 * d + 2, lanes] = out[2 * f : 2 * f + 2]

    def forward(n, get):
        def first(i, carry):
            lanes = pl.ds(pl.multiple_of(i * tile_len, tile_len), tile_len)
            out = dot_nt(get(lanes).astype(jnp.bfloat16), uf[:, lanes])
            half = out.shape[1] // 2
            coef[pl.ds(pl.multiple_of(i * 8, 8), 8), :] = out[:, :half] + turned(out[:, half:], 1.0)
            return carry

        lax.fori_loop(0, tiles_here, first, 0)
        kept = (coef[...] * keep_f[...]).astype(jnp.bfloat16)
        kj, ki = ranks * tiles, ranks * tiles_here
        row = lax.broadcasted_iota(jnp.int32, (kj, 2 * ki), 0)
        col = lax.broadcasted_iota(jnp.int32, (kj, 2 * ki), 1)
        same_k = row // tiles == (col % ki) // tiles_here
        shift = row % tiles - col // ki
        row_i = lax.broadcasted_iota(jnp.int32, (8 * tiles_here, 2 * ki), 0) // 8
        col_i = lax.broadcasted_iota(jnp.int32, (8 * tiles_here, 2 * ki), 1) % tiles_here
        own = row_i == col_i

        def second(jp, carry):
            pick = jnp.where(same_k & (shift == 2 * jp), 1.0, 0.0).astype(jnp.bfloat16)
            wide = jnp.where(own, dot(kept, pick), 0.0)
            both = jnp.sum(wide.reshape(tiles_here, 8, 2 * ki), axis=0)
            for jj in range(2):
                part = both[:, jj * ki : (jj + 1) * ki]
                lhs = jnp.concatenate([part, turned(part, 1.0)], axis=1).astype(jnp.bfloat16)
                at = pl.multiple_of((2 * jp + jj) * tile_len, tile_len)
                out = dot(lhs, vf[:, pl.ds(at, tile_len)])
                block = jp // (tiles_here // 2)
                at = pl.multiple_of((2 * jp + jj - block * tiles_here) * tile_len, tile_len)
                ybuf[n, block, 0, :, pl.ds(at, tile_len)] = out[:4]
                ybuf[n, block, 1, :, pl.ds(at, tile_len)] = out[4:]
            return carry

        lax.fori_loop(0, tiles // 2, second, 0)
        copies = [
            send(ybuf.at[n, device["recv"], device["sub"]], yrecv.at[n, k], device)
            for k, device in enumerate(near)
        ]
        for copy in copies:
            copy.wait()
        total = ybuf[n, x, c]
        for k in range(len(near)):
            total = total + yrecv[n, k]
        pg[n, z] = total
        for copy in gather_freq(pg.at[n]):
            copy.wait()

    def chunks(step):
        def one(k, carry):
            step(pl.ds(pl.multiple_of(k * CHUNK, CHUNK), CHUNK))
            return carry

        lax.fori_loop(0, lanes_all // CHUNK, one, 0)

    def start_spec(lanes):
        for d in range(2):
            put_spectrum(0, d, lanes, spectrum_chunk(table_wide[...], foc[d, :, lanes]))

    chunks(start_spec)
    zsum[...] = reduce_freq(0)
    send(zsum, zother, {"sub": 1 - c}).wait()

    def spec_rows(lanes):
        mine, other = zsum[:, lanes], zother[:, lanes]
        first, last = jnp.where(c == 0, mine, other), jnp.where(c == 0, other, mine)
        return jnp.concatenate([first, last], axis=0)

    forward(0, spec_rows)

    def windowed(lanes):
        for d in range(2):
            signal = signal_chunk(table_tall[...], seen_rows(pg.at[0], d, lanes, nf))
            t = tids[...]
            inside = (start[d : d + 1, lanes] <= t) & (t < end[d : d + 1, lanes])
            kept = jnp.where(inside, obs[d, :, lanes] - signal, 0.0)
            put_spectrum(1, d, lanes, spectrum_chunk(table_wide[...], kept))

    chunks(windowed)
    zg[x, c] = reduce_freq(1)
    for copy in [send(zg.at[x, c], zg.at[x, c], device) for device in near]:
        copy.wait()

    ki, kj = ranks * tiles_here, ranks * tiles

    def adjoint_first(j, carry):
        block = j // tiles_here
        at = pl.multiple_of((j - block * tiles_here) * tile_len, tile_len)
        rows = jnp.concatenate(
            [zg[block, 0, :, pl.ds(at, tile_len)], zg[block, 1, :, pl.ds(at, tile_len)]], axis=0
        )
        at = pl.multiple_of(j * tile_len, tile_len)
        out = dot_nt(rows.astype(jnp.bfloat16), vf[:, pl.ds(at, tile_len)])
        adj[pl.ds(pl.multiple_of(j * 8, 8), 8), :] = out[:, :ki] + turned(out[:, ki:], -1.0)
        return carry

    lax.fori_loop(0, tiles, adjoint_first, 0)
    kept_a = (adj[...] * keep_a[...]).astype(jnp.bfloat16)
    row = lax.broadcasted_iota(jnp.int32, (ki, kj), 0)
    col = lax.broadcasted_iota(jnp.int32, (ki, kj), 1)
    same_k = row // tiles_here == col // tiles
    row_i = row % tiles_here
    own_a = (
        lax.broadcasted_iota(jnp.int32, (8 * tiles, kj), 0) // 8
        == lax.broadcasted_iota(jnp.int32, (8 * tiles, kj), 1) % tiles
    )

    def adjoint_second(i, carry):
        pick = jnp.where(same_k & (row_i == i), 1.0, 0.0).astype(jnp.bfloat16)
        wide = jnp.where(own_a, dot(kept_a, pick), 0.0)
        part = jnp.sum(wide.reshape(tiles, 8, kj), axis=0)
        lhs = jnp.concatenate([part, turned(part, -1.0)], axis=1).astype(jnp.bfloat16)
        lanes = pl.ds(pl.multiple_of(i * tile_len, tile_len), tile_len)
        ga[:, lanes] = dot(lhs, uf[:, lanes])
        return carry

    lax.fori_loop(0, tiles_here, adjoint_second, 0)
    send(ga, gother, {"sub": 1 - c}).wait()
    total = ga[...] + gother[...]
    gg[z] = jnp.where(c == 0, total[:4], total[4:])
    late = gather_freq(gg)
    forward(1, lambda lanes: (ga[:, lanes] + gother[:, lanes]) * gain)
    p_out[...] = pg[0] + pg[1]
    for copy in late:
        copy.wait()
    g_out[...] = gg[...]


def final_kernel(nf, foc, obs, start, end, tids, table_tall, p, g, new_foc, new_res):
    def run(d):
        lanes = slice(None)
        new_foc[0] = foc[0] + relax_step * signal_chunk(
            table_tall[...], seen_rows(g, d, lanes, nf)
        )
        signal = signal_chunk(table_tall[...], seen_rows(p, d, lanes, nf))
        t = tids[...]
        inside = (start[d : d + 1, :] <= t) & (t < end[d : d + 1, :])
        new_res[0] = obs[0] - jnp.where(inside, signal, 0.0)

    for d in range(2):
        pl.when(pl.program_id(0) == d)(functools.partial(run, d))


def split_table(table):
    high = lax.reduce_precision(table, 8, 7)
    low = lax.reduce_precision(table - high, 8, 7)
    return high.astype(jnp.bfloat16), low.astype(jnp.bfloat16)


def fast_body(focusing, observed, recv_factor, source_factor, tile_ranks, window_start, window_end):
    nf = lax.axis_size("freq")
    ranks, tiles = recv_factor.shape[2:4]
    tiles_here = source_factor.shape[3]
    half_foc, local_t, lanes = focusing.shape
    tile_len = lanes // tiles_here
    cos_table, sin_table = dft_tables(nf, NT)
    table = jnp.stack([cos_table, -sin_table], axis=1).reshape(2 * nf, NT)
    table = lax.dynamic_slice_in_dim(table, lax.axis_index("freq") * local_t, local_t, 1)
    high, low = split_table(table)
    table_wide = jnp.concatenate(
        [jnp.concatenate([high, high], 1), jnp.concatenate([low, low], 1)], 0
    )
    table_tall = jnp.concatenate([high, high, low, low], 0).T
    tids = (lax.axis_index("freq") * local_t + jnp.arange(local_t, dtype=jnp.int32))[:, None]
    rank_ids = lax.axis_index("sub") * ranks + jnp.arange(ranks, dtype=jnp.int32)
    held = tile_ranks[0]
    keep_f = (rank_ids[None, :, None] < held[:, None, :]).astype(jnp.float32)
    keep_f = jnp.repeat(keep_f.reshape(tiles_here, ranks * tiles), 8, axis=0)
    keep_a = (rank_ids[None, :, None] < held.T[:, None, :]).astype(jnp.float32)
    keep_a = jnp.repeat(keep_a.reshape(tiles, ranks * tiles_here), 8, axis=0)
    uf = recv_factor.reshape(2 * ranks * tiles, lanes)
    vf = source_factor.reshape(2 * ranks * tiles_here, tiles * tile_len)
    gain = (0.5 * NT) * float(nf * NT) ** (-0.5)
    f32 = jnp.float32
    spectra = jax.ShapeDtypeStruct((nf, 4, lanes), f32)
    p, g = pl.pallas_call(
        functools.partial(core_kernel, nf, tiles, tiles_here, ranks, tile_len, gain),
        out_shape=(spectra, spectra),
        in_specs=[pl.BlockSpec(memory_space=pltpu.VMEM)] * 11,
        out_specs=(pl.BlockSpec(memory_space=pltpu.VMEM),) * 2,
        scratch_shapes=[
            pltpu.VMEM((2, nf, 4, lanes), f32),
            pltpu.VMEM((2, nf - 1, 4, lanes), f32),
            pltpu.VMEM((4, lanes), f32),
            pltpu.VMEM((4, lanes), f32),
            pltpu.VMEM((8 * tiles_here, ranks * tiles), f32),
            pltpu.VMEM((2, 2, 2, 4, lanes), f32),
            pltpu.VMEM((2, 3, 4, lanes), f32),
            pltpu.VMEM((2, nf, 4, lanes), f32),
            pltpu.VMEM((2, 2, 4, lanes), f32),
            pltpu.VMEM((8 * tiles, ranks * tiles_here), f32),
            pltpu.VMEM((8, lanes), f32),
            pltpu.VMEM((8, lanes), f32),
            pltpu.VMEM((nf, 4, lanes), f32),
            pltpu.SemaphoreType.DMA((5 * (nf - 1) + 11,)),
            pltpu.SemaphoreType.DMA((5 * (nf - 1) + 11,)),
        ],
        compiler_params=pltpu.CompilerParams(
            collective_id=0, has_side_effects=True, vmem_limit_bytes=48 * 2**20
        ),
        name="spectra",
    )(focusing, observed, uf, vf, keep_f, keep_a, window_start, window_end, tids, table_wide, table_tall)
    width = 1024
    signal_spec = pl.BlockSpec((1, local_t, width), lambda d, k: (d, 0, k))
    edge_spec = pl.BlockSpec((half_foc, width), lambda d, k: (0, k))
    spectra_spec = pl.BlockSpec((nf, 4, width), lambda d, k: (0, 0, k))
    return pl.pallas_call(
        functools.partial(final_kernel, nf),
        grid=(half_foc, lanes // width),
        out_shape=(jax.ShapeDtypeStruct(focusing.shape, f32),) * 2,
        in_specs=[
            signal_spec, signal_spec, edge_spec, edge_spec,
            pl.BlockSpec(tids.shape, lambda d, k: (0, 0)),
            pl.BlockSpec(table_tall.shape, lambda d, k: (0, 0)),
            spectra_spec, spectra_spec,
        ],
        out_specs=(signal_spec,) * 2,
        compiler_params=pltpu.CompilerParams(vmem_limit_bytes=32 * 2**20),
        name="update",
    )(focusing, observed, window_start, window_end, tids, table_tall, p, g)


def fits(focusing, recv_factor, source_factor):
    bands, ranks, tiles = recv_factor.shape[1:4]
    tiles_here = source_factor.shape[3]
    half_foc, local_t, lanes = focusing.shape
    return (
        (lax.axis_size("freq"), lax.axis_size("recv"), lax.axis_size("sub")) == (4, 2, 2)
        and (bands, half_foc, local_t) == (1, 2, 128)
        and (ranks * tiles_here) % 128 == 0
        and lanes // tiles_here == 256
        and tiles == 2 * tiles_here
        and lanes % 1024 == 0
    )


def chosen(focusing, observed, recv_factor, source_factor, *rest):
    form = fast_body if fits(focusing, recv_factor, source_factor) else body
    return form(focusing, observed, recv_factor, source_factor, *rest)


def solution(mesh):
    placed = (
        P(("group", "sub"), "freq", "recv"),
        P(("group", "sub"), "freq", "recv"),
        P("group", "freq", "sub", None, "recv"),
        P("group", "freq", "sub", "recv", None),
        P(("group", "freq"), "recv", None),
        P(("group", "sub"), "recv"),
        P(("group", "sub"), "recv"),
    )
    return jax.shard_map(
        chosen,
        mesh=mesh,
        in_specs=placed,
        out_specs=(P(("group", "sub"), "freq", "recv"), P(("group", "sub"), "freq", "recv")),
        check_vma=False,
    )
```

```python
import functools
import math

import jax
import jax.numpy as jnp
from jax import lax
from jax.experimental import pallas as pl
from jax.experimental.pallas import tpu as pltpu
from jax.sharding import PartitionSpec as P

NT = 512


first_bin = 4
relax_step = 1.0
highest = lax.Precision.HIGHEST


def dft_tables(count, samples):
    freqs = first_bin + jnp.arange(count, dtype=jnp.int32)
    sample_ids = jnp.arange(samples, dtype=jnp.int32)
    turns = (freqs[:, None] * sample_ids[None, :] % samples).astype(jnp.float32)
    phase = turns * (2.0 * math.pi / samples)
    weight = float(count * samples) ** (-0.25)
    return (jnp.cos(phase) * weight, jnp.sin(phase) * weight)


def signal_of(spectrum, cos_table, sin_table):
    return jnp.einsum("ft,fqr->qtr", cos_table, spectrum[0], precision=highest) - jnp.einsum(
        "ft,fqr->qtr", sin_table, spectrum[1], precision=highest
    )


def contract(form, left, right):
    return jnp.einsum(form, left, right, preferred_element_type=jnp.float32)


def body(focusing, observed, recv_factor, source_factor, tile_ranks, window_start, window_end):
    freq_count = lax.axis_size("freq")
    recv_count = lax.axis_size("recv")
    sub_count = lax.axis_size("sub")
    bands = recv_factor.shape[1]
    rank_cols = recv_factor.shape[2]
    tiles_all = recv_factor.shape[3]
    tiles_here = source_factor.shape[3]
    half_foc, local_t, rec_block = focusing.shape
    tile_len = rec_block // tiles_here
    col_tiles = tiles_all // recv_count
    cos_table, sin_table = dft_tables(bands * freq_count, NT)
    rank_ids = lax.axis_index("sub") * rank_cols + jnp.arange(rank_cols, dtype=jnp.int32)
    rank_keep = (
        rank_ids[None, :, None, None] < jnp.transpose(tile_ranks, (0, 2, 1))[:, None, :, :]
    ).astype(jnp.float32)
    recv_tiles = recv_factor.reshape(2, bands, rank_cols, tiles_all, tiles_here, tile_len)
    recv_blocks = recv_factor.reshape(
        2, bands, rank_cols, recv_count, col_tiles, tiles_here, tile_len
    )
    source_blocks = source_factor.reshape(
        2, bands, rank_cols, tiles_here, recv_count, col_tiles, tile_len
    )
    keep_blocks = rank_keep.reshape(bands, rank_cols, recv_count, col_tiles, tiles_here)

    def forward(spec_half):
        gathered = lax.all_gather(spec_half, "sub", axis=2, tiled=True)
        tiles = gathered.reshape(2, bands, sub_count * half_foc, tiles_here, tile_len)
        real_part = contract("fkjin,fqin->fkjiq", recv_tiles[0], tiles[0]) - contract(
            "fkjin,fqin->fkjiq", recv_tiles[1], tiles[1]
        )
        imag_part = contract("fkjin,fqin->fkjiq", recv_tiles[0], tiles[1]) + contract(
            "fkjin,fqin->fkjiq", recv_tiles[1], tiles[0]
        )
        coeffs = (jnp.stack([real_part, imag_part]) * rank_keep[None, :, :, :, :, None]).astype(
            jnp.bfloat16
        )
        coeffs = coeffs.reshape(
            2, bands, rank_cols, recv_count, col_tiles, tiles_here, sub_count, half_foc
        )
        out_real = contract("fkibjn,fkbjiud->fbudjn", source_blocks[0], coeffs[0]) - contract(
            "fkibjn,fkbjiud->fbudjn", source_blocks[1], coeffs[1]
        )
        out_imag = contract("fkibjn,fkbjiud->fbudjn", source_blocks[0], coeffs[1]) + contract(
            "fkibjn,fkbjiud->fbudjn", source_blocks[1], coeffs[0]
        )
        partial_term = jnp.stack([out_real, out_imag]).reshape(
            2, bands, recv_count * sub_count * half_foc, rec_block
        )
        return lax.psum_scatter(partial_term, ("recv", "sub"), scatter_dimension=2, tiled=True)

    traces, seen = (focusing, observed)
    sample_ids = lax.axis_index("freq") * local_t + jnp.arange(local_t, dtype=jnp.int32)
    window = (
        (window_start[:, None, :] <= sample_ids[None, :, None])
        & (sample_ids[None, :, None] < window_end[:, None, :])
    ).astype(jnp.float32)

    local_cos = lax.dynamic_slice_in_dim(cos_table, lax.axis_index("freq") * local_t, local_t, 1)
    local_sin = lax.dynamic_slice_in_dim(sin_table, lax.axis_index("freq") * local_t, local_t, 1)

    def to_spectrum(signal):
        real_part = jnp.einsum("ft,qtr->fqr", local_cos, signal, precision=highest)
        imag_part = -jnp.einsum("ft,qtr->fqr", local_sin, signal, precision=highest)
        whole = lax.psum_scatter(
            jnp.stack([real_part, imag_part]), "freq", scatter_dimension=1, tiled=True
        )
        return whole.astype(jnp.bfloat16)

    def to_signal(spectrum):
        return signal_of(
            lax.all_gather(spectrum, "freq", axis=1, tiled=True), local_cos, local_sin
        )

    predicted = to_signal(forward(to_spectrum(traces)))
    residual = seen - window * predicted
    gathered = lax.all_gather(to_spectrum(window * residual), ("recv", "sub"), axis=2, tiled=True)
    tiles = gathered.reshape(2, bands, recv_count, sub_count, half_foc, col_tiles, tile_len)
    real_part = contract("fkibjn,fbudjn->fkbjiud", source_blocks[0], tiles[0]) + contract(
        "fkibjn,fbudjn->fkbjiud", source_blocks[1], tiles[1]
    )
    imag_part = contract("fkibjn,fbudjn->fkbjiud", source_blocks[0], tiles[1]) - contract(
        "fkibjn,fbudjn->fkbjiud", source_blocks[1], tiles[0]
    )
    coeffs = (
        jnp.stack([real_part, imag_part]) * keep_blocks[None, :, :, :, :, :, None, None]
    ).astype(jnp.bfloat16)
    out_real = contract("fkbjim,fkbjiud->fudim", recv_blocks[0], coeffs[0]) + contract(
        "fkbjim,fkbjiud->fudim", recv_blocks[1], coeffs[1]
    )
    out_imag = contract("fkbjim,fkbjiud->fudim", recv_blocks[0], coeffs[1]) - contract(
        "fkbjim,fkbjiud->fudim", recv_blocks[1], coeffs[0]
    )
    partial_term = jnp.stack([out_real, out_imag]).reshape(
        2, bands, sub_count * half_foc, rec_block
    )
    grad_spec = lax.psum_scatter(partial_term, "sub", scatter_dimension=2, tiled=True)
    gradient = to_signal(grad_spec)
    gain = (0.5 * NT) * float(bands * freq_count * NT) ** (-0.5)
    image = window * to_signal(forward((grad_spec * gain).astype(jnp.bfloat16)))
    new_focus = traces + relax_step * gradient
    new_residual = residual - relax_step * image
    return (new_focus, new_residual)


CHUNK = 512


def dot(a, b):
    return lax.dot_general(a, b, (((1,), (0,)), ((), ())), preferred_element_type=jnp.float32)


def dot_nt(a, b):
    return lax.dot_general(a, b, (((1,), (1,)), ((), ())), preferred_element_type=jnp.float32)


def turned(x, sign):
    row = lax.broadcasted_iota(jnp.int32, x.shape, 0)
    up = pltpu.roll(x, x.shape[0] - 1, 0)
    down = pltpu.roll(x, 1, 0)
    return jnp.where(row % 2 == 0, -sign * up, sign * down)


def halves(x):
    high = x.astype(jnp.bfloat16)
    return high, (x - high.astype(jnp.float32)).astype(jnp.bfloat16)


def packed(x):
    w = x.shape[1] // 4
    return jnp.concatenate([x[:, k * w : (k + 1) * w] for k in range(4)], axis=0).astype(jnp.bfloat16)


def unpacked(x):
    y = x.astype(jnp.float32)
    return jnp.concatenate([y[4 * k : 4 * k + 4] for k in range(4)], axis=1)


def spectrum_chunk(table_wide, v):
    out = dot(table_wide, jnp.concatenate(halves(v), axis=0))
    rows = out.shape[0] // 2
    return out[:rows] + out[rows:]


def signal_chunk(table_tall, p):
    high, low = halves(p)
    high, low = high.astype(jnp.float32), low.astype(jnp.float32)
    return dot(table_tall, jnp.concatenate([high, low, high, low], axis=0).astype(jnp.bfloat16))


def seen_rows(ref, d, lanes, count):
    return jnp.concatenate([ref[f, 2 * d : 2 * d + 2, lanes] for f in range(count)], axis=0)


def core_kernel(
    nf, tiles, tiles_here, ranks, tile_len, gain,
    foc_in, obs_in, uf_in, vf_in, keep_f, keep_a, start, end, tids, table_wide, table_tall,
    p_out, g_out,
    sp, zrecv, zsum, zother, coef, ybuf, yrecv, pg, zg, adj, ga, gother,
    spb, subb, pgb, zgb, ggb, foc, obs, uf, vf, load_sem,
    send_sem, recv_sem,
):
    z, x, c = lax.axis_index("freq"), lax.axis_index("recv"), lax.axis_index("sub")
    lanes_all = tiles_here * tile_len
    peers = [(dx, dc) for dx in range(2) for dc in range(2) if dx + dc]
    part = lanes_all // 4
    loads = [
        pltpu.make_async_copy(
            foc_in.at[:, :, pl.ds(k * part, part)],
            foc.at[:, :, pl.ds(k * part, part)],
            load_sem.at[k],
        )
        for k in range(4)
    ]
    for k, (src, dst) in enumerate([(uf_in, uf), (vf_in, vf), (obs_in, obs)]):
        loads.append(pltpu.make_async_copy(src, dst, load_sem.at[4 + k]))
    for load in loads:
        load.start()
    zs = [{"freq": lax.rem(z + k, nf)} for k in range(1, nf)]
    near = [{"recv": x + dx - 2 * dx * x, "sub": c + dc - 2 * dc * c} for dx, dc in peers]
    barrier = pltpu.get_barrier_semaphore()
    for device in zs + near:
        pl.semaphore_signal(
            barrier, inc=1, device_id=device, device_id_type=pl.DeviceIdType.MESH
        )
    pl.semaphore_wait(barrier, nf - 1 + len(peers))
    used = [0]

    def send(src, dst, device):
        n = used[0]
        used[0] += 1
        copy = pltpu.make_async_remote_copy(
            src_ref=src, dst_ref=dst, send_sem=send_sem.at[n], recv_sem=recv_sem.at[n],
            device_id=device, device_id_type=pl.DeviceIdType.MESH,
        )
        copy.start()
        return copy

    def reduce_freq(n):
        for f in range(nf):
            spb[n, f] = packed(sp[n, f])
        copies = [
            send(spb.at[n, zs[k]["freq"]], zrecv.at[n, k], zs[k]) for k in range(nf - 1)
        ]
        for copy in copies:
            copy.wait()
        total = sp[n, z]
        for k in range(nf - 1):
            total = total + unpacked(zrecv[n, k])
        return total

    def gather_freq(buf):
        return [send(buf.at[z], buf.at[z], zs[k]) for k in range(nf - 1)]

    def put_spectrum(n, d, lanes, out):
        for f in range(nf):
            sp[n, f, 2 * d : 2 * d + 2, lanes] = out[2 * f : 2 * f + 2]

    def forward(n, get):
        def first(i, carry):
            lanes = pl.ds(pl.multiple_of(i * tile_len, tile_len), tile_len)
            out = dot_nt(get(lanes).astype(jnp.bfloat16), uf[:, lanes])
            half = out.shape[1] // 2
            coef[pl.ds(pl.multiple_of(i * 8, 8), 8), :] = out[:, :half] + turned(out[:, half:], 1.0)
            return carry

        lax.fori_loop(0, tiles_here, first, 0, unroll=16)
        kept = (coef[...] * keep_f[...]).astype(jnp.bfloat16)
        kj, ki = ranks * tiles, ranks * tiles_here
        row = lax.broadcasted_iota(jnp.int32, (kj, 2 * ki), 0)
        col = lax.broadcasted_iota(jnp.int32, (kj, 2 * ki), 1)
        same_k = row // tiles == (col % ki) // tiles_here
        shift = row % tiles - col // ki
        row_i = lax.broadcasted_iota(jnp.int32, (8 * tiles_here, 2 * ki), 0) // 8
        col_i = lax.broadcasted_iota(jnp.int32, (8 * tiles_here, 2 * ki), 1) % tiles_here
        own = row_i == col_i

        def second(jp, carry):
            pick = jnp.where(same_k & (shift == 2 * jp), 1.0, 0.0).astype(jnp.bfloat16)
            wide = jnp.where(own, dot(kept, pick), 0.0)
            both = jnp.sum(wide.reshape(tiles_here, 8, 2 * ki), axis=0)
            for jj in range(2):
                part = both[:, jj * ki : (jj + 1) * ki]
                lhs = jnp.concatenate([part, turned(part, 1.0)], axis=1).astype(jnp.bfloat16)
                at = pl.multiple_of((2 * jp + jj) * tile_len, tile_len)
                out = dot(lhs, vf[:, pl.ds(at, tile_len)])
                block = jp // (tiles_here // 2)
                at = pl.multiple_of((2 * jp + jj - block * tiles_here) * tile_len, tile_len)
                ybuf[n, block, 0, :, pl.ds(at, tile_len)] = out[:4]
                ybuf[n, block, 1, :, pl.ds(at, tile_len)] = out[4:]
            return carry

        lax.fori_loop(0, tiles // 2, second, 0, unroll=8)
        copies = [
            send(ybuf.at[n, device["recv"], device["sub"]], yrecv.at[n, k], device)
            for k, device in enumerate(near)
        ]
        for copy in copies:
            copy.wait()
        total = ybuf[n, x, c]
        for k in range(len(near)):
            total = total + yrecv[n, k]
        pgb[n, z] = packed(total)
        for copy in gather_freq(pgb.at[n]):
            copy.wait()
        for f in range(nf):
            pg[n, f] = unpacked(pgb[n, f])

    def chunks(step, first=0, last=lanes_all // CHUNK):
        def one(k, carry):
            step(pl.ds(pl.multiple_of(k * CHUNK, CHUNK), CHUNK))
            return carry

        lax.fori_loop(first, last, one, 0, unroll=2)

    def start_spec(lanes):
        for d in range(2):
            put_spectrum(0, d, lanes, spectrum_chunk(table_wide[...], foc[d, :, lanes]))

    for k in range(4):
        loads[k].wait()
        chunks(start_spec, k * part // CHUNK, (k + 1) * part // CHUNK)
    subb[0] = packed(reduce_freq(0))
    send(subb.at[0], subb.at[1], {"sub": 1 - c}).wait()
    zsum[...] = unpacked(subb[0])
    zother[...] = unpacked(subb[1])

    def spec_rows(lanes):
        mine, other = zsum[:, lanes], zother[:, lanes]
        first, last = jnp.where(c == 0, mine, other), jnp.where(c == 0, other, mine)
        return jnp.concatenate([first, last], axis=0)

    loads[4].wait()
    loads[5].wait()
    forward(0, spec_rows)
    loads[6].wait()

    def windowed(lanes):
        for d in range(2):
            signal = signal_chunk(table_tall[...], seen_rows(pg.at[0], d, lanes, nf))
            t = tids[...]
            inside = (start[d : d + 1, lanes] <= t) & (t < end[d : d + 1, lanes])
            kept = jnp.where(inside, obs[d, :, lanes] - signal, 0.0)
            put_spectrum(1, d, lanes, spectrum_chunk(table_wide[...], kept))

    chunks(windowed)
    zgb[x, c] = packed(reduce_freq(1))
    for copy in [send(zgb.at[x, c], zgb.at[x, c], device) for device in near]:
        copy.wait()
    for block in range(2):
        for half in range(2):
            zg[block, half] = unpacked(zgb[block, half])

    ki, kj = ranks * tiles_here, ranks * tiles

    def adjoint_first(j, carry):
        block = j // tiles_here
        at = pl.multiple_of((j - block * tiles_here) * tile_len, tile_len)
        rows = jnp.concatenate(
            [zg[block, 0, :, pl.ds(at, tile_len)], zg[block, 1, :, pl.ds(at, tile_len)]], axis=0
        )
        at = pl.multiple_of(j * tile_len, tile_len)
        out = dot_nt(rows.astype(jnp.bfloat16), vf[:, pl.ds(at, tile_len)])
        adj[pl.ds(pl.multiple_of(j * 8, 8), 8), :] = out[:, :ki] + turned(out[:, ki:], -1.0)
        return carry

    lax.fori_loop(0, tiles, adjoint_first, 0, unroll=16)
    kept_a = (adj[...] * keep_a[...]).astype(jnp.bfloat16)
    row = lax.broadcasted_iota(jnp.int32, (ki, kj), 0)
    col = lax.broadcasted_iota(jnp.int32, (ki, kj), 1)
    same_k = row // tiles_here == col // tiles
    row_i = row % tiles_here
    own_a = (
        lax.broadcasted_iota(jnp.int32, (8 * tiles, kj), 0) // 8
        == lax.broadcasted_iota(jnp.int32, (8 * tiles, kj), 1) % tiles
    )

    def adjoint_second(i, carry):
        pick = jnp.where(same_k & (row_i == i), 1.0, 0.0).astype(jnp.bfloat16)
        wide = jnp.where(own_a, dot(kept_a, pick), 0.0)
        part = jnp.sum(wide.reshape(tiles, 8, kj), axis=0)
        lhs = jnp.concatenate([part, turned(part, -1.0)], axis=1).astype(jnp.bfloat16)
        lanes = pl.ds(pl.multiple_of(i * tile_len, tile_len), tile_len)
        ga[:, lanes] = dot(lhs, uf[:, lanes])
        return carry

    lax.fori_loop(0, tiles_here, adjoint_second, 0, unroll=8)
    send(ga, gother, {"sub": 1 - c}).wait()
    total = ga[...] + gother[...]
    ggb[z] = packed(jnp.where(c == 0, total[:4], total[4:]))
    late = gather_freq(ggb)
    forward(1, lambda lanes: (ga[:, lanes] + gother[:, lanes]) * gain)
    p_out[...] = pg[0] + pg[1]
    for copy in late:
        copy.wait()
    for f in range(nf):
        g_out[f] = unpacked(ggb[f])


def final_kernel(nf, foc, obs, start, end, tids, table_tall, p, g, new_foc, new_res):
    def run(d):
        lanes = slice(None)
        new_foc[0] = foc[0] + relax_step * signal_chunk(
            table_tall[...], seen_rows(g, d, lanes, nf)
        )
        signal = signal_chunk(table_tall[...], seen_rows(p, d, lanes, nf))
        t = tids[...]
        inside = (start[d : d + 1, :] <= t) & (t < end[d : d + 1, :])
        new_res[0] = obs[0] - jnp.where(inside, signal, 0.0)

    for d in range(2):
        pl.when(pl.program_id(0) == d)(functools.partial(run, d))


def split_table(table):
    high = lax.reduce_precision(table, 8, 7)
    low = lax.reduce_precision(table - high, 8, 7)
    return high.astype(jnp.bfloat16), low.astype(jnp.bfloat16)


def fast_body(focusing, observed, recv_factor, source_factor, tile_ranks, window_start, window_end):
    nf = lax.axis_size("freq")
    ranks, tiles = recv_factor.shape[2:4]
    tiles_here = source_factor.shape[3]
    half_foc, local_t, lanes = focusing.shape
    tile_len = lanes // tiles_here
    cos_table, sin_table = dft_tables(nf, NT)
    table = jnp.stack([cos_table, -sin_table], axis=1).reshape(2 * nf, NT)
    table = lax.dynamic_slice_in_dim(table, lax.axis_index("freq") * local_t, local_t, 1)
    high, low = split_table(table)
    table_wide = jnp.concatenate(
        [jnp.concatenate([high, high], 1), jnp.concatenate([low, low], 1)], 0
    )
    table_tall = jnp.concatenate([high, high, low, low], 0).T
    tids = (lax.axis_index("freq") * local_t + jnp.arange(local_t, dtype=jnp.int32))[:, None]
    rank_ids = lax.axis_index("sub") * ranks + jnp.arange(ranks, dtype=jnp.int32)
    held = tile_ranks[0]
    keep_f = (rank_ids[None, :, None] < held[:, None, :]).astype(jnp.float32)
    keep_f = jnp.repeat(keep_f.reshape(tiles_here, ranks * tiles), 8, axis=0)
    keep_a = (rank_ids[None, :, None] < held.T[:, None, :]).astype(jnp.float32)
    keep_a = jnp.repeat(keep_a.reshape(tiles, ranks * tiles_here), 8, axis=0)
    uf = recv_factor.reshape(2 * ranks * tiles, lanes)
    vf = source_factor.reshape(2 * ranks * tiles_here, tiles * tile_len)
    gain = (0.5 * NT) * float(nf * NT) ** (-0.5)
    f32 = jnp.float32
    spectra = jax.ShapeDtypeStruct((nf, 4, lanes), f32)
    p, g = pl.pallas_call(
        functools.partial(core_kernel, nf, tiles, tiles_here, ranks, tile_len, gain),
        out_shape=(spectra, spectra),
        in_specs=[pl.BlockSpec(memory_space=pl.ANY)] * 4
        + [pl.BlockSpec(memory_space=pltpu.VMEM)] * 7,
        out_specs=(pl.BlockSpec(memory_space=pltpu.VMEM),) * 2,
        scratch_shapes=[
            pltpu.VMEM((2, nf, 4, lanes), f32),
            pltpu.VMEM((2, nf - 1, 16, lanes // 4), jnp.bfloat16),
            pltpu.VMEM((4, lanes), f32),
            pltpu.VMEM((4, lanes), f32),
            pltpu.VMEM((8 * tiles_here, ranks * tiles), f32),
            pltpu.VMEM((2, 2, 2, 4, lanes), f32),
            pltpu.VMEM((2, 3, 4, lanes), f32),
            pltpu.VMEM((2, nf, 4, lanes), f32),
            pltpu.VMEM((2, 2, 4, lanes), f32),
            pltpu.VMEM((8 * tiles, ranks * tiles_here), f32),
            pltpu.VMEM((8, lanes), f32),
            pltpu.VMEM((8, lanes), f32),
            pltpu.VMEM((2, nf, 16, lanes // 4), jnp.bfloat16),
            pltpu.VMEM((2, 16, lanes // 4), jnp.bfloat16),
            pltpu.VMEM((2, nf, 16, lanes // 4), jnp.bfloat16),
            pltpu.VMEM((2, 2, 16, lanes // 4), jnp.bfloat16),
            pltpu.VMEM((nf, 16, lanes // 4), jnp.bfloat16),
            pltpu.VMEM(focusing.shape, f32),
            pltpu.VMEM(observed.shape, f32),
            pltpu.VMEM(uf.shape, jnp.bfloat16),
            pltpu.VMEM(vf.shape, jnp.bfloat16),
            pltpu.SemaphoreType.DMA((7,)),
            pltpu.SemaphoreType.DMA((5 * (nf - 1) + 11,)),
            pltpu.SemaphoreType.DMA((5 * (nf - 1) + 11,)),
        ],
        compiler_params=pltpu.CompilerParams(
            collective_id=0, has_side_effects=True, vmem_limit_bytes=48 * 2**20
        ),
        name="spectra",
    )(focusing, observed, uf, vf, keep_f, keep_a, window_start, window_end, tids, table_wide, table_tall)
    width = 1024
    signal_spec = pl.BlockSpec((1, local_t, width), lambda d, k: (d, 0, k))
    edge_spec = pl.BlockSpec((half_foc, width), lambda d, k: (0, k))
    spectra_spec = pl.BlockSpec((nf, 4, width), lambda d, k: (0, 0, k))
    return pl.pallas_call(
        functools.partial(final_kernel, nf),
        grid=(half_foc, lanes // width),
        out_shape=(jax.ShapeDtypeStruct(focusing.shape, f32),) * 2,
        in_specs=[
            signal_spec, signal_spec, edge_spec, edge_spec,
            pl.BlockSpec(tids.shape, lambda d, k: (0, 0)),
            pl.BlockSpec(table_tall.shape, lambda d, k: (0, 0)),
            spectra_spec, spectra_spec,
        ],
        out_specs=(signal_spec,) * 2,
        compiler_params=pltpu.CompilerParams(vmem_limit_bytes=32 * 2**20),
        name="update",
    )(focusing, observed, window_start, window_end, tids, table_tall, p, g)


def fits(focusing, recv_factor, source_factor):
    bands, ranks, tiles = recv_factor.shape[1:4]
    tiles_here = source_factor.shape[3]
    half_foc, local_t, lanes = focusing.shape
    return (
        (lax.axis_size("freq"), lax.axis_size("recv"), lax.axis_size("sub")) == (4, 2, 2)
        and (bands, half_foc, local_t) == (1, 2, 128)
        and (ranks * tiles_here) % 128 == 0
        and lanes // tiles_here == 256
        and tiles == 2 * tiles_here
        and lanes % 1024 == 0
    )


def chosen(focusing, observed, recv_factor, source_factor, *rest):
    form = fast_body if fits(focusing, recv_factor, source_factor) else body
    return form(focusing, observed, recv_factor, source_factor, *rest)


def solution(mesh):
    placed = (
        P(("group", "sub"), "freq", "recv"),
        P(("group", "sub"), "freq", "recv"),
        P("group", "freq", "sub", None, "recv"),
        P("group", "freq", "sub", "recv", None),
        P(("group", "freq"), "recv", None),
        P(("group", "sub"), "recv"),
        P(("group", "sub"), "recv"),
    )
    return jax.shard_map(
        chosen,
        mesh=mesh,
        in_specs=placed,
        out_specs=(P(("group", "sub"), "freq", "recv"), P(("group", "sub"), "freq", "recv")),
        check_vma=False,
    )
```

```python
import functools
import math

import jax
import jax.numpy as jnp
from jax import lax
from jax.experimental import pallas as pl
from jax.experimental.pallas import tpu as pltpu
from jax.sharding import PartitionSpec as P

NT = 512


first_bin = 4
relax_step = 1.0
highest = lax.Precision.HIGHEST


def dft_tables(count, samples):
    freqs = first_bin + jnp.arange(count, dtype=jnp.int32)
    sample_ids = jnp.arange(samples, dtype=jnp.int32)
    turns = (freqs[:, None] * sample_ids[None, :] % samples).astype(jnp.float32)
    phase = turns * (2.0 * math.pi / samples)
    weight = float(count * samples) ** (-0.25)
    return (jnp.cos(phase) * weight, jnp.sin(phase) * weight)


def signal_of(spectrum, cos_table, sin_table):
    return jnp.einsum("ft,fqr->qtr", cos_table, spectrum[0], precision=highest) - jnp.einsum(
        "ft,fqr->qtr", sin_table, spectrum[1], precision=highest
    )


def contract(form, left, right):
    return jnp.einsum(form, left, right, preferred_element_type=jnp.float32)


def body(focusing, observed, recv_factor, source_factor, tile_ranks, window_start, window_end):
    freq_count = lax.axis_size("freq")
    recv_count = lax.axis_size("recv")
    sub_count = lax.axis_size("sub")
    bands = recv_factor.shape[1]
    rank_cols = recv_factor.shape[2]
    tiles_all = recv_factor.shape[3]
    tiles_here = source_factor.shape[3]
    half_foc, local_t, rec_block = focusing.shape
    tile_len = rec_block // tiles_here
    col_tiles = tiles_all // recv_count
    cos_table, sin_table = dft_tables(bands * freq_count, NT)
    rank_ids = lax.axis_index("sub") * rank_cols + jnp.arange(rank_cols, dtype=jnp.int32)
    rank_keep = (
        rank_ids[None, :, None, None] < jnp.transpose(tile_ranks, (0, 2, 1))[:, None, :, :]
    ).astype(jnp.float32)
    recv_tiles = recv_factor.reshape(2, bands, rank_cols, tiles_all, tiles_here, tile_len)
    recv_blocks = recv_factor.reshape(
        2, bands, rank_cols, recv_count, col_tiles, tiles_here, tile_len
    )
    source_blocks = source_factor.reshape(
        2, bands, rank_cols, tiles_here, recv_count, col_tiles, tile_len
    )
    keep_blocks = rank_keep.reshape(bands, rank_cols, recv_count, col_tiles, tiles_here)

    def forward(spec_half):
        gathered = lax.all_gather(spec_half, "sub", axis=2, tiled=True)
        tiles = gathered.reshape(2, bands, sub_count * half_foc, tiles_here, tile_len)
        real_part = contract("fkjin,fqin->fkjiq", recv_tiles[0], tiles[0]) - contract(
            "fkjin,fqin->fkjiq", recv_tiles[1], tiles[1]
        )
        imag_part = contract("fkjin,fqin->fkjiq", recv_tiles[0], tiles[1]) + contract(
            "fkjin,fqin->fkjiq", recv_tiles[1], tiles[0]
        )
        coeffs = (jnp.stack([real_part, imag_part]) * rank_keep[None, :, :, :, :, None]).astype(
            jnp.bfloat16
        )
        coeffs = coeffs.reshape(
            2, bands, rank_cols, recv_count, col_tiles, tiles_here, sub_count, half_foc
        )
        out_real = contract("fkibjn,fkbjiud->fbudjn", source_blocks[0], coeffs[0]) - contract(
            "fkibjn,fkbjiud->fbudjn", source_blocks[1], coeffs[1]
        )
        out_imag = contract("fkibjn,fkbjiud->fbudjn", source_blocks[0], coeffs[1]) + contract(
            "fkibjn,fkbjiud->fbudjn", source_blocks[1], coeffs[0]
        )
        partial_term = jnp.stack([out_real, out_imag]).reshape(
            2, bands, recv_count * sub_count * half_foc, rec_block
        )
        return lax.psum_scatter(partial_term, ("recv", "sub"), scatter_dimension=2, tiled=True)

    traces, seen = (focusing, observed)
    sample_ids = lax.axis_index("freq") * local_t + jnp.arange(local_t, dtype=jnp.int32)
    window = (
        (window_start[:, None, :] <= sample_ids[None, :, None])
        & (sample_ids[None, :, None] < window_end[:, None, :])
    ).astype(jnp.float32)

    local_cos = lax.dynamic_slice_in_dim(cos_table, lax.axis_index("freq") * local_t, local_t, 1)
    local_sin = lax.dynamic_slice_in_dim(sin_table, lax.axis_index("freq") * local_t, local_t, 1)

    def to_spectrum(signal):
        real_part = jnp.einsum("ft,qtr->fqr", local_cos, signal, precision=highest)
        imag_part = -jnp.einsum("ft,qtr->fqr", local_sin, signal, precision=highest)
        whole = lax.psum_scatter(
            jnp.stack([real_part, imag_part]), "freq", scatter_dimension=1, tiled=True
        )
        return whole.astype(jnp.bfloat16)

    def to_signal(spectrum):
        return signal_of(
            lax.all_gather(spectrum, "freq", axis=1, tiled=True), local_cos, local_sin
        )

    predicted = to_signal(forward(to_spectrum(traces)))
    residual = seen - window * predicted
    gathered = lax.all_gather(to_spectrum(window * residual), ("recv", "sub"), axis=2, tiled=True)
    tiles = gathered.reshape(2, bands, recv_count, sub_count, half_foc, col_tiles, tile_len)
    real_part = contract("fkibjn,fbudjn->fkbjiud", source_blocks[0], tiles[0]) + contract(
        "fkibjn,fbudjn->fkbjiud", source_blocks[1], tiles[1]
    )
    imag_part = contract("fkibjn,fbudjn->fkbjiud", source_blocks[0], tiles[1]) - contract(
        "fkibjn,fbudjn->fkbjiud", source_blocks[1], tiles[0]
    )
    coeffs = (
        jnp.stack([real_part, imag_part]) * keep_blocks[None, :, :, :, :, :, None, None]
    ).astype(jnp.bfloat16)
    out_real = contract("fkbjim,fkbjiud->fudim", recv_blocks[0], coeffs[0]) + contract(
        "fkbjim,fkbjiud->fudim", recv_blocks[1], coeffs[1]
    )
    out_imag = contract("fkbjim,fkbjiud->fudim", recv_blocks[0], coeffs[1]) - contract(
        "fkbjim,fkbjiud->fudim", recv_blocks[1], coeffs[0]
    )
    partial_term = jnp.stack([out_real, out_imag]).reshape(
        2, bands, sub_count * half_foc, rec_block
    )
    grad_spec = lax.psum_scatter(partial_term, "sub", scatter_dimension=2, tiled=True)
    gradient = to_signal(grad_spec)
    gain = (0.5 * NT) * float(bands * freq_count * NT) ** (-0.5)
    image = window * to_signal(forward((grad_spec * gain).astype(jnp.bfloat16)))
    new_focus = traces + relax_step * gradient
    new_residual = residual - relax_step * image
    return (new_focus, new_residual)


CHUNK = 512


def dot(a, b):
    return lax.dot_general(a, b, (((1,), (0,)), ((), ())), preferred_element_type=jnp.float32)


def dot_nt(a, b):
    return lax.dot_general(a, b, (((1,), (1,)), ((), ())), preferred_element_type=jnp.float32)


def turned(x, sign):
    row = lax.broadcasted_iota(jnp.int32, x.shape, 0)
    up = pltpu.roll(x, x.shape[0] - 1, 0)
    down = pltpu.roll(x, 1, 0)
    return jnp.where(row % 2 == 0, -sign * up, sign * down)


def halves(x):
    high = x.astype(jnp.bfloat16)
    return high, (x - high.astype(jnp.float32)).astype(jnp.bfloat16)


def packed(x):
    w = x.shape[1] // 4
    return jnp.concatenate([x[:, k * w : (k + 1) * w] for k in range(4)], axis=0).astype(jnp.bfloat16)


def unpacked(x):
    y = x.astype(jnp.float32)
    return jnp.concatenate([y[4 * k : 4 * k + 4] for k in range(4)], axis=1)


def spectrum_chunk(table_wide, v):
    out = dot(table_wide, jnp.concatenate(halves(v), axis=0))
    rows = out.shape[0] // 2
    return out[:rows] + out[rows:]


def signal_chunk(table_tall, p):
    high, low = halves(p)
    high, low = high.astype(jnp.float32), low.astype(jnp.float32)
    return dot(table_tall, jnp.concatenate([high, low, high, low], axis=0).astype(jnp.bfloat16))


def seen_rows(ref, d, lanes, count):
    return jnp.concatenate([ref[f, 2 * d : 2 * d + 2, lanes] for f in range(count)], axis=0)


def core_kernel(
    nf, tiles, tiles_here, ranks, tile_len, gain,
    foc_in, obs_in, uf_in, vf_in, keep_f, keep_a, start, end, tids, table_wide, table_tall,
    p_out, g_out,
    sp, zrecv, zsum, zother, coef, ybuf, yrecv, pg, zg, adj, ga, gother,
    subb, pgb, zgb, ggb, foc, obs, uf, vf, load_sem,
    send_sem, recv_sem,
):
    z, x, c = lax.axis_index("freq"), lax.axis_index("recv"), lax.axis_index("sub")
    lanes_all = tiles_here * tile_len
    peers = [(dx, dc) for dx in range(2) for dc in range(2) if dx + dc]
    part = lanes_all // 4
    loads = [
        pltpu.make_async_copy(
            foc_in.at[:, :, pl.ds(k * part, part)],
            foc.at[:, :, pl.ds(k * part, part)],
            load_sem.at[k],
        )
        for k in range(4)
    ]
    for k, (src, dst) in enumerate([(uf_in, uf), (vf_in, vf), (obs_in, obs)]):
        loads.append(pltpu.make_async_copy(src, dst, load_sem.at[4 + k]))
    for load in loads:
        load.start()
    zs = [{"freq": lax.rem(z + k, nf)} for k in range(1, nf)]
    near = [{"recv": x + dx - 2 * dx * x, "sub": c + dc - 2 * dc * c} for dx, dc in peers]
    barrier = pltpu.get_barrier_semaphore()
    for device in zs + near:
        pl.semaphore_signal(
            barrier, inc=1, device_id=device, device_id_type=pl.DeviceIdType.MESH
        )
    pl.semaphore_wait(barrier, nf - 1 + len(peers))
    used = [0]

    def send(src, dst, device):
        n = used[0]
        used[0] += 1
        copy = pltpu.make_async_remote_copy(
            src_ref=src, dst_ref=dst, send_sem=send_sem.at[n], recv_sem=recv_sem.at[n],
            device_id=device, device_id_type=pl.DeviceIdType.MESH,
        )
        copy.start()
        return copy

    def reduce_freq(n):
        copies = [
            send(sp.at[n, zs[k]["freq"]], zrecv.at[n, k], zs[k]) for k in range(nf - 1)
        ]
        for copy in copies:
            copy.wait()
        total = sp[n, z]
        for k in range(nf - 1):
            total = total + zrecv[n, k]
        return total

    def gather_freq(buf):
        return [send(buf.at[z], buf.at[z], zs[k]) for k in range(nf - 1)]

    def put_spectrum(n, d, lanes, out):
        for f in range(nf):
            sp[n, f, 2 * d : 2 * d + 2, lanes] = out[2 * f : 2 * f + 2]

    def forward(n, get):
        def first(i, carry):
            lanes = pl.ds(pl.multiple_of(i * tile_len, tile_len), tile_len)
            out = dot_nt(get(lanes).astype(jnp.bfloat16), uf[:, lanes])
            half = out.shape[1] // 2
            coef[pl.ds(pl.multiple_of(i * 8, 8), 8), :] = out[:, :half] + turned(out[:, half:], 1.0)
            return carry

        lax.fori_loop(0, tiles_here, first, 0, unroll=16)
        kept = (coef[...] * keep_f[...]).astype(jnp.bfloat16)
        kj, ki = ranks * tiles, ranks * tiles_here
        row = lax.broadcasted_iota(jnp.int32, (kj, 2 * ki), 0)
        col = lax.broadcasted_iota(jnp.int32, (kj, 2 * ki), 1)
        same_k = row // tiles == (col % ki) // tiles_here
        shift = row % tiles - col // ki
        row_i = lax.broadcasted_iota(jnp.int32, (8 * tiles_here, 2 * ki), 0) // 8
        col_i = lax.broadcasted_iota(jnp.int32, (8 * tiles_here, 2 * ki), 1) % tiles_here
        own = row_i == col_i

        def second(jp, carry):
            pick = jnp.where(same_k & (shift == 2 * jp), 1.0, 0.0).astype(jnp.bfloat16)
            wide = jnp.where(own, dot(kept, pick), 0.0)
            both = jnp.sum(wide.reshape(tiles_here, 8, 2 * ki), axis=0)
            for jj in range(2):
                part = both[:, jj * ki : (jj + 1) * ki]
                lhs = jnp.concatenate([part, turned(part, 1.0)], axis=1).astype(jnp.bfloat16)
                at = pl.multiple_of((2 * jp + jj) * tile_len, tile_len)
                out = dot(lhs, vf[:, pl.ds(at, tile_len)])
                block = jp // (tiles_here // 2)
                at = pl.multiple_of((2 * jp + jj - block * tiles_here) * tile_len, tile_len)
                ybuf[n, block, 0, :, pl.ds(at, tile_len)] = out[:4]
                ybuf[n, block, 1, :, pl.ds(at, tile_len)] = out[4:]
            return carry

        lax.fori_loop(0, tiles // 2, second, 0, unroll=8)
        copies = [
            send(ybuf.at[n, device["recv"], device["sub"]], yrecv.at[n, k], device)
            for k, device in enumerate(near)
        ]
        for copy in copies:
            copy.wait()
        total = ybuf[n, x, c]
        for k in range(len(near)):
            total = total + yrecv[n, k]
        pgb[n, z] = packed(total)
        for copy in gather_freq(pgb.at[n]):
            copy.wait()
        for f in range(nf):
            pg[n, f] = unpacked(pgb[n, f])

    def chunks(step, first=0, last=lanes_all // CHUNK):
        def one(k, carry):
            step(pl.ds(pl.multiple_of(k * CHUNK, CHUNK), CHUNK))
            return carry

        lax.fori_loop(first, last, one, 0, unroll=2)

    def start_spec(lanes):
        for d in range(2):
            put_spectrum(0, d, lanes, spectrum_chunk(table_wide[...], foc[d, :, lanes]))

    for k in range(4):
        loads[k].wait()
        chunks(start_spec, k * part // CHUNK, (k + 1) * part // CHUNK)
    subb[0] = packed(reduce_freq(0))
    send(subb.at[0], subb.at[1], {"sub": 1 - c}).wait()
    zsum[...] = unpacked(subb[0])
    zother[...] = unpacked(subb[1])

    def spec_rows(lanes):
        mine, other = zsum[:, lanes], zother[:, lanes]
        first, last = jnp.where(c == 0, mine, other), jnp.where(c == 0, other, mine)
        return jnp.concatenate([first, last], axis=0)

    loads[4].wait()
    loads[5].wait()
    forward(0, spec_rows)
    loads[6].wait()

    def windowed(lanes):
        for d in range(2):
            signal = signal_chunk(table_tall[...], seen_rows(pg.at[0], d, lanes, nf))
            t = tids[...]
            inside = (start[d : d + 1, lanes] <= t) & (t < end[d : d + 1, lanes])
            kept = jnp.where(inside, obs[d, :, lanes] - signal, 0.0)
            put_spectrum(1, d, lanes, spectrum_chunk(table_wide[...], kept))

    chunks(windowed)
    zgb[x, c] = packed(reduce_freq(1))
    for copy in [send(zgb.at[x, c], zgb.at[x, c], device) for device in near]:
        copy.wait()
    for block in range(2):
        for half in range(2):
            zg[block, half] = unpacked(zgb[block, half])

    ki, kj = ranks * tiles_here, ranks * tiles

    def adjoint_first(j, carry):
        block = j // tiles_here
        at = pl.multiple_of((j - block * tiles_here) * tile_len, tile_len)
        rows = jnp.concatenate(
            [zg[block, 0, :, pl.ds(at, tile_len)], zg[block, 1, :, pl.ds(at, tile_len)]], axis=0
        )
        at = pl.multiple_of(j * tile_len, tile_len)
        out = dot_nt(rows.astype(jnp.bfloat16), vf[:, pl.ds(at, tile_len)])
        adj[pl.ds(pl.multiple_of(j * 8, 8), 8), :] = out[:, :ki] + turned(out[:, ki:], -1.0)
        return carry

    lax.fori_loop(0, tiles, adjoint_first, 0, unroll=16)
    kept_a = (adj[...] * keep_a[...]).astype(jnp.bfloat16)
    row = lax.broadcasted_iota(jnp.int32, (ki, kj), 0)
    col = lax.broadcasted_iota(jnp.int32, (ki, kj), 1)
    same_k = row // tiles_here == col // tiles
    row_i = row % tiles_here
    own_a = (
        lax.broadcasted_iota(jnp.int32, (8 * tiles, kj), 0) // 8
        == lax.broadcasted_iota(jnp.int32, (8 * tiles, kj), 1) % tiles
    )

    def adjoint_second(i, carry):
        pick = jnp.where(same_k & (row_i == i), 1.0, 0.0).astype(jnp.bfloat16)
        wide = jnp.where(own_a, dot(kept_a, pick), 0.0)
        part = jnp.sum(wide.reshape(tiles, 8, kj), axis=0)
        lhs = jnp.concatenate([part, turned(part, -1.0)], axis=1).astype(jnp.bfloat16)
        lanes = pl.ds(pl.multiple_of(i * tile_len, tile_len), tile_len)
        ga[:, lanes] = dot(lhs, uf[:, lanes])
        return carry

    lax.fori_loop(0, tiles_here, adjoint_second, 0, unroll=8)
    send(ga, gother, {"sub": 1 - c}).wait()
    total = ga[...] + gother[...]
    ggb[z] = jnp.where(c == 0, total[:4], total[4:])
    late = gather_freq(ggb)
    forward(1, lambda lanes: (ga[:, lanes] + gother[:, lanes]) * gain)
    p_out[...] = pg[0] + pg[1]
    for copy in late:
        copy.wait()
    for f in range(nf):
        g_out[f] = ggb[f]


def final_kernel(nf, foc, obs, start, end, tids, table_tall, p, g, new_foc, new_res):
    def run(d):
        lanes = slice(None)
        new_foc[0] = foc[0] + relax_step * signal_chunk(
            table_tall[...], seen_rows(g, d, lanes, nf)
        )
        signal = signal_chunk(table_tall[...], seen_rows(p, d, lanes, nf))
        t = tids[...]
        inside = (start[d : d + 1, :] <= t) & (t < end[d : d + 1, :])
        new_res[0] = obs[0] - jnp.where(inside, signal, 0.0)

    for d in range(2):
        pl.when(pl.program_id(0) == d)(functools.partial(run, d))


def split_table(table):
    high = lax.reduce_precision(table, 8, 7)
    low = lax.reduce_precision(table - high, 8, 7)
    return high.astype(jnp.bfloat16), low.astype(jnp.bfloat16)


def fast_body(focusing, observed, recv_factor, source_factor, tile_ranks, window_start, window_end):
    nf = lax.axis_size("freq")
    ranks, tiles = recv_factor.shape[2:4]
    tiles_here = source_factor.shape[3]
    half_foc, local_t, lanes = focusing.shape
    tile_len = lanes // tiles_here
    cos_table, sin_table = dft_tables(nf, NT)
    table = jnp.stack([cos_table, -sin_table], axis=1).reshape(2 * nf, NT)
    table = lax.dynamic_slice_in_dim(table, lax.axis_index("freq") * local_t, local_t, 1)
    high, low = split_table(table)
    table_wide = jnp.concatenate(
        [jnp.concatenate([high, high], 1), jnp.concatenate([low, low], 1)], 0
    )
    table_tall = jnp.concatenate([high, high, low, low], 0).T
    tids = (lax.axis_index("freq") * local_t + jnp.arange(local_t, dtype=jnp.int32))[:, None]
    rank_ids = lax.axis_index("sub") * ranks + jnp.arange(ranks, dtype=jnp.int32)
    held = tile_ranks[0]
    keep_f = (rank_ids[None, :, None] < held[:, None, :]).astype(jnp.float32)
    keep_f = jnp.repeat(keep_f.reshape(tiles_here, ranks * tiles), 8, axis=0)
    keep_a = (rank_ids[None, :, None] < held.T[:, None, :]).astype(jnp.float32)
    keep_a = jnp.repeat(keep_a.reshape(tiles, ranks * tiles_here), 8, axis=0)
    uf = recv_factor.reshape(2 * ranks * tiles, lanes)
    vf = source_factor.reshape(2 * ranks * tiles_here, tiles * tile_len)
    gain = (0.5 * NT) * float(nf * NT) ** (-0.5)
    f32 = jnp.float32
    spectra = jax.ShapeDtypeStruct((nf, 4, lanes), f32)
    p, g = pl.pallas_call(
        functools.partial(core_kernel, nf, tiles, tiles_here, ranks, tile_len, gain),
        out_shape=(spectra, spectra),
        in_specs=[pl.BlockSpec(memory_space=pl.ANY)] * 4
        + [pl.BlockSpec(memory_space=pltpu.VMEM)] * 7,
        out_specs=(pl.BlockSpec(memory_space=pltpu.VMEM),) * 2,
        scratch_shapes=[
            pltpu.VMEM((2, nf, 4, lanes), f32),
            pltpu.VMEM((2, nf - 1, 4, lanes), f32),
            pltpu.VMEM((4, lanes), f32),
            pltpu.VMEM((4, lanes), f32),
            pltpu.VMEM((8 * tiles_here, ranks * tiles), f32),
            pltpu.VMEM((2, 2, 2, 4, lanes), f32),
            pltpu.VMEM((2, 3, 4, lanes), f32),
            pltpu.VMEM((2, nf, 4, lanes), f32),
            pltpu.VMEM((2, 2, 4, lanes), f32),
            pltpu.VMEM((8 * tiles, ranks * tiles_here), f32),
            pltpu.VMEM((8, lanes), f32),
            pltpu.VMEM((8, lanes), f32),
            pltpu.VMEM((2, 16, lanes // 4), jnp.bfloat16),
            pltpu.VMEM((2, nf, 16, lanes // 4), jnp.bfloat16),
            pltpu.VMEM((2, 2, 16, lanes // 4), jnp.bfloat16),
            pltpu.VMEM((nf, 4, lanes), f32),
            pltpu.VMEM(focusing.shape, f32),
            pltpu.VMEM(observed.shape, f32),
            pltpu.VMEM(uf.shape, jnp.bfloat16),
            pltpu.VMEM(vf.shape, jnp.bfloat16),
            pltpu.SemaphoreType.DMA((7,)),
            pltpu.SemaphoreType.DMA((5 * (nf - 1) + 11,)),
            pltpu.SemaphoreType.DMA((5 * (nf - 1) + 11,)),
        ],
        compiler_params=pltpu.CompilerParams(
            collective_id=0, has_side_effects=True, vmem_limit_bytes=60 * 2**20
        ),
        name="spectra",
    )(focusing, observed, uf, vf, keep_f, keep_a, window_start, window_end, tids, table_wide, table_tall)
    width = 1024
    signal_spec = pl.BlockSpec((1, local_t, width), lambda d, k: (d, 0, k))
    edge_spec = pl.BlockSpec((half_foc, width), lambda d, k: (0, k))
    spectra_spec = pl.BlockSpec((nf, 4, width), lambda d, k: (0, 0, k))
    return pl.pallas_call(
        functools.partial(final_kernel, nf),
        grid=(half_foc, lanes // width),
        out_shape=(jax.ShapeDtypeStruct(focusing.shape, f32),) * 2,
        in_specs=[
            signal_spec, signal_spec, edge_spec, edge_spec,
            pl.BlockSpec(tids.shape, lambda d, k: (0, 0)),
            pl.BlockSpec(table_tall.shape, lambda d, k: (0, 0)),
            spectra_spec, spectra_spec,
        ],
        out_specs=(signal_spec,) * 2,
        compiler_params=pltpu.CompilerParams(vmem_limit_bytes=32 * 2**20),
        name="update",
    )(focusing, observed, window_start, window_end, tids, table_tall, p, g)


def fits(focusing, recv_factor, source_factor):
    bands, ranks, tiles = recv_factor.shape[1:4]
    tiles_here = source_factor.shape[3]
    half_foc, local_t, lanes = focusing.shape
    return (
        (lax.axis_size("freq"), lax.axis_size("recv"), lax.axis_size("sub")) == (4, 2, 2)
        and (bands, half_foc, local_t) == (1, 2, 128)
        and (ranks * tiles_here) % 128 == 0
        and lanes // tiles_here == 256
        and tiles == 2 * tiles_here
        and lanes % 1024 == 0
    )


def chosen(focusing, observed, recv_factor, source_factor, *rest):
    form = fast_body if fits(focusing, recv_factor, source_factor) else body
    return form(focusing, observed, recv_factor, source_factor, *rest)


def solution(mesh):
    placed = (
        P(("group", "sub"), "freq", "recv"),
        P(("group", "sub"), "freq", "recv"),
        P("group", "freq", "sub", None, "recv"),
        P("group", "freq", "sub", "recv", None),
        P(("group", "freq"), "recv", None),
        P(("group", "sub"), "recv"),
        P(("group", "sub"), "recv"),
    )
    return jax.shard_map(
        chosen,
        mesh=mesh,
        in_specs=placed,
        out_specs=(P(("group", "sub"), "freq", "recv"), P(("group", "sub"), "freq", "recv")),
        check_vma=False,
    )
```
